32 devices in a mesh: groups: 2 (over y), aux: 8 (over z, x), occ: 1, vir: 2 (over core).
Axes of the slice: x: 2, y: 2, z: 4, core: 2. Of those that a mesh axis runs over, the one named last changes fastest.
Arguments:
- integrals: bfloat16 [2496, 16, 512], P(('aux', 'occ'), 'groups', 'vir'), parts along dimension 1, may hold values from -0.59765625 to 0.59765625
- virt_energy: float32 [30720], replicated, may hold values from 0.5 to 4
- occ_energy: float32 [16], P('groups'), parts along dimension 0, may hold values from -1.5 to -0.3
- domain: int32 [16, 4], P('groups'), parts along dimension 0, may hold values from 0 to 239
- partners: int32 [16, 2], P('groups'), parts along dimension 0, may hold values from 0 to 7, all different within a row
- pair_count: int32 [16], P('groups'), parts along dimension 0, may hold values from 1 to 2, 10 in all
Outputs:
- gamma: bfloat16 [2496, 16, 512], P(('aux', 'occ'), 'groups', 'vir'), parts along dimension 1
The draws below stay inside these ranges and needn't reach their ends.
There are 2 independent parts, one for each index of `groups`. The reference program is written for one: setup_inputs(seed, part) draws one part's arguments, and reference() takes and returns one part's arrays. A program takes and returns all parts, laid end to end along the dimension named above; an argument that names none is the same for every part. Nothing has to cross between parts.
Inputs may be any that keep to these rules, and one draw needn't show every extreme that they name: Each row names 2 different partners; every orbital is some orbital's partner. `pair_count`: some orbital has all 2 slots live.
All inputs are finite; a program needn't handle non-finite values.
Results may differ from the reference program's by a relative error of at most 0.005.
Values may be sent and summed in bfloat16 or wider, within the bound.
A program may use at most 128 MiB of HBM per device.

```python
import math
import jax
import jax.numpy as jnp
import numpy as np
from jax import lax

VB = 128
NDOM = 4
NVB = 240
MAXP = 2
NOCC = 8
NAUX = 2496
DOMV = 512
VIRT = 30720


def touch_ends(array, key, low, high):
    extent = array.shape
    place = [jax.random.randint(jax.random.fold_in(key, axis), (), 0, extent[axis]) for axis in range(len(extent))]
    array = array.at[tuple(place)].set(low)
    longest = extent.index(max(extent))
    place[longest] = (place[longest] + 1) % extent[longest]
    return array.at[tuple(place)].set(high)


def block_levels(rng, dims, split, least, largest):
    factor_of, own = 1.0, jax.random.fold_in(rng, 6)
    for position, blocks in split:
        draws = jnp.exp(jax.random.uniform(jax.random.fold_in(own, position), (blocks,), jnp.float32, least / len(split), largest / len(split)))
        factor_of = factor_of * jnp.repeat(draws, dims[position] // blocks).reshape([-1 if axis == position else 1 for axis in range(len(dims))])
    return factor_of


def distinct(rng, rows, count, top, lift):
    ranking = jax.random.permutation(jax.random.fold_in(rng, 1), count)
    boost = ranking
    for power in range(3):
        boost = boost * boost // count
    boost = boost * lift // count
    tickets = jax.random.randint(jax.random.fold_in(rng, 2), (rows, count), 0, 4096) + boost
    fixed_rows = jax.random.permutation(jax.random.fold_in(rng, 3), rows)[jnp.arange(count) % rows]
    tickets = jnp.where(jnp.arange(rows)[:, None] == fixed_rows[None, :], 1 << 14, tickets)
    priority = tickets * count + jnp.arange(count)
    return lax.top_k(priority.astype(jnp.int32), top)[1].astype(jnp.int32)


def profile(amount, total, limit, skew):
    weights = [(1 << 20) // math.isqrt(standing ** skew) + 1 for standing in range(2, amount + 1)]
    spare, holding = total - limit - (amount - 1), [1] * (amount - 1)
    while spare > 0:
        free = [i for i in range(amount - 1) if holding[i] < limit]
        mass, budget = sum([weights[i] for i in free]), spare
        for i in free:
            addition = min(limit - holding[i], max(1, budget * weights[i] // mass), spare)
            holding[i] = holding[i] + addition
            spare = spare - addition
    return np.array([limit] + holding)


def ragged_sizes(rng, number_of, total, bound, slope):
    if number_of == 2:
        one = jax.random.randint(rng, (), max(1, total - bound), min(bound, total - 1) + 1)
        return jnp.stack([one, total - one])
    tallies = jnp.asarray(profile(number_of, total, bound, slope), jnp.int32)
    couples = (number_of - 1) // 2
    source_of, taker = tallies[1:1 + 2 * couples:2], tallies[2:2 + 2 * couples:2]
    room = jnp.minimum(source_of - 1, bound - taker)
    passed = jax.random.randint(jax.random.fold_in(rng, 1), (couples,), 0, 1 << 20) % (room + 1)
    tallies = tallies.at[1:1 + 2 * couples:2].set(source_of - passed).at[2:2 + 2 * couples:2].set(taker + passed)
    return tallies[jax.random.permutation(jax.random.fold_in(rng, 2), number_of)]


def centred(key, dims, spread, limit, shards=(), held_as=jnp.bfloat16):
    entries = spread * jax.random.normal(key, dims, jnp.float32)
    if shards:
        entries = entries * block_levels(key, dims, shards, -0.22, 0.18)
    return jnp.clip(entries, -limit, limit).astype(held_as)


def setup_inputs(seed: int = 0, part: int = 0) -> dict:
    arg_keys = jax.random.split(jax.random.key(seed), 7)
    own_keys = jax.random.split(jax.random.fold_in(arg_keys[6], part), 7)
    return {
        "integrals": centred(own_keys[0], (NAUX, NOCC, DOMV), 0.1, 0.59765625, ((0, 8), (2, 2))),
        "virt_energy": jnp.clip(jax.random.uniform(arg_keys[1], (VIRT,), jnp.float32, 0.5, 4.0), 0.5, 4.0),
        "occ_energy": jnp.clip(jax.random.uniform(own_keys[2], (NOCC,), jnp.float32, -1.5, -0.3), -1.5, -0.3),
        "domain": touch_ends(jax.random.randint(own_keys[3], (NOCC, NDOM), 0, NVB), jax.random.fold_in(own_keys[3], 1), 0, NVB - 1).astype(jnp.int32),
        "partners": distinct(own_keys[4], NOCC, NOCC, MAXP, 4096),
        "pair_count": ragged_sizes(own_keys[5], NOCC, NOCC * MAXP * 5 // 8, MAXP, 0).astype(jnp.int32),
    }


def reference(integrals, virt_energy, occ_energy, domain, partners, pair_count):
    eps_dom = virt_energy.reshape(NVB, VB)[domain].reshape(NOCC, DOMV)
    slots = jnp.arange(MAXP, dtype=jnp.int32)

    def per_orbital(orbital):
        chosen = partners[orbital]
        partner_rows = jnp.take(integrals, chosen, axis=1).astype(jnp.float32)
        own_rows = jnp.take(integrals, orbital, axis=1).astype(jnp.float32)
        pair_sums = jnp.einsum("rsa,rb->sab", partner_rows, own_rows)
        denominator = (eps_dom[chosen][:, :, None] + eps_dom[orbital][None, None, :]) - occ_energy[chosen][:, None, None] - occ_energy[orbital]
        live_slot = (slots < pair_count[orbital]).astype(jnp.float32)
        amplitude = (-(pair_sums / denominator) * live_slot[:, None, None]).astype(jnp.bfloat16)
        return jnp.einsum("rsa,sab->rb", partner_rows, amplitude.astype(jnp.float32)).astype(jnp.bfloat16)

    gamma_rows = lax.map(per_orbital, jnp.arange(NOCC, dtype=jnp.int32))
    return jnp.transpose(gamma_rows, (1, 0, 2))
```

```python
import functools
import math

import jax
import jax.numpy as jnp
from jax import lax
from jax.experimental import pallas as pl
from jax.experimental.pallas import tpu as pltpu
from jax.sharding import PartitionSpec as P

VB = 128
MESH = pl.DeviceIdType.MESH
BF16 = jnp.bfloat16
F32 = jnp.float32


def grid_of(aux_count, occ_count):
    if occ_count == 1:
        return aux_count // 2, 2
    return aux_count, occ_count


def ring_place(z, x, Z, X):
    comb = x * (Z - 1) + jnp.where(x % 2 == 0, z - 1, Z - 1 - z)
    return jnp.where(z == 0, X * (Z - 1) + X - 1 - x, comb)


def ring_point(p, Z, X):
    x = p // (Z - 1)
    r = p % (Z - 1)
    comb_z = jnp.where(x % 2 == 0, r + 1, Z - 1 - r)
    back = p >= X * (Z - 1)
    return jnp.where(back, 0, comb_z), jnp.where(back, X - 1 - (p - X * (Z - 1)), x)


def steps(low, high, body):
    if high - low <= 6:
        for t in range(low, high):
            body(t)
    elif high > low:
        lax.fori_loop(low, high, lambda t, c: (body(t), c)[1], 0)


def kernel(
    aux_count, occ_count, pair_total,
    partners, domain, count, occ_energy, virt, own,
    out,
    peer, sums, amp, sent, came, turned, second,
    peer_sem, rs_send, rs_recv, ag_send, ag_recv,
):
    nocc, aux_rows, half_width = own.shape
    width = 2 * half_width
    Z, X = grid_of(aux_count, occ_count)
    N = Z * X
    H = N // 2
    rows = pair_total * width // N
    sub_rows = (-(-rows // 32) * 16, rows - (-(-rows // 32) * 16))
    sub_off = (0, sub_rows[0])
    group, aux, occ, v = (lax.axis_index(a) for a in ("groups", "aux", "occ", "vir"))
    if occ_count == 1:
        z, x = aux // X, aux % X
    else:
        z, x = aux, occ
    p = ring_place(z, x, Z, X)

    def device(q):
        qz, qx = ring_point(lax.rem(q + N, N), Z, X)
        if occ_count == 1:
            return (group, qz * X + qx, 0, v)
        return (group, qz, qx, v)

    target = (device(p + 1), device(p - 1))
    other = (group, aux, occ, 1 - v)
    barrier = pltpu.get_barrier_semaphore()
    for d in (*target, other):
        pl.semaphore_signal(barrier, inc=1, device_id=d, device_id_type=MESH)
    pl.semaphore_wait(barrier, 3)

    swap = pltpu.make_async_remote_copy(
        src_ref=own, dst_ref=peer, send_sem=peer_sem.at[0], recv_sem=peer_sem.at[1],
        device_id=other, device_id_type=MESH,
    )
    swap.start()

    ahead = []
    running = jnp.int32(0)
    for j in range(nocc):
        ahead.append(running)
        running = running + count[j] - 1
    def holds(j, e):
        apart = ahead[j] - e
        return (count[j] - 1) * jnp.maximum(1 - jnp.maximum(apart, -apart), 0)

    extras = pair_total - nocc
    pair_j = [jnp.int32(j) for j in range(nocc)]
    pair_i = [partners[j, 0] for j in range(nocc)]
    for e in range(extras):
        pair_j.append(sum(holds(j, e) * j for j in range(nocc)))
        pair_i.append(sum(holds(j, e) * partners[j, 1] for j in range(nocc)))

    def mul_t(a, b):
        return lax.dot_general(a, b, (((0,), (0,)), ((), ())), preferred_element_type=F32)

    for k in range(pair_total):
        at = pl.multiple_of(k * width + v * half_width, half_width)
        sums[pl.ds(at, half_width), :] = mul_t(own[pair_i[k]], own[pair_j[k]])
    swap.wait()
    for k in range(pair_total):
        at = pl.multiple_of(k * width + (1 - v) * half_width, half_width)
        sums[pl.ds(at, half_width), :] = mul_t(peer[pair_i[k]], own[pair_j[k]])

    def chunk_rows(c, sub):
        c = lax.rem(c + 2 * N, N)
        return pl.ds(pl.multiple_of(c * rows + sub_off[sub], 16), sub_rows[sub])

    def part(sub):
        return pl.ds(sub_off[sub], sub_rows[sub])

    def rs_copy(d, t, sub):
        return pltpu.make_async_remote_copy(
            src_ref=sent.at[d, t, part(sub), :], dst_ref=came.at[d, t, part(sub), :],
            send_sem=rs_send.at[d, t, sub], recv_sem=rs_recv.at[d, t, sub],
            device_id=target[d], device_id_type=MESH,
        )

    def rs_step(d, t, sub, add):
        sign = 1 - 2 * d
        value = sums[chunk_rows(p + sign * (H - t), sub), :]
        if add:
            rs_copy(d, t - 1, sub).wait_recv()
            value = value + came[d, t - 1, part(sub), :].astype(F32)
        sent[d, t, part(sub), :] = value.astype(BF16)
        rs_copy(d, t, sub).start()

    rs_step(0, 0, 0, False)
    rs_step(1, 0, 1, False)
    rs_step(0, 1, 1, False)
    rs_step(1, 1, 0, False)
    rs_step(0, 1, 0, True)
    rs_step(1, 1, 1, True)

    def rs_body(t):
        rs_step(0, t, 1, True)
        rs_step(1, t, 0, True)
        rs_step(0, t, 0, True)
        rs_step(1, t, 1, True)

    steps(2, H, rs_body)

    def ag_copy(d, t, sub):
        where = chunk_rows(p - (1 - 2 * d) * t, sub)
        return pltpu.make_async_remote_copy(
            src_ref=amp.at[where, :], dst_ref=amp.at[where, :],
            send_sem=ag_send.at[d, t, sub], recv_sem=ag_recv.at[d, t, sub],
            device_id=target[d], device_id_type=MESH,
        )

    piece = math.gcd(math.gcd(sub_rows[0], sub_rows[1]), VB)
    blocks = half_width // VB

    def amplitude(sub):
        rs_copy(0, H - 1, sub).wait_recv()
        rs_copy(1, H - 1, sub).wait_recv()
        for q in range(sub_rows[sub] // piece):
            local = sub_off[sub] + q * piece
            row = pl.multiple_of(p * rows + local, piece)
            k = row // width
            a = row % width
            j = jnp.int32(0)
            i = jnp.int32(0)
            for m in range(pair_total):
                same = (k == m).astype(jnp.int32)
                j = j + same * pair_j[m]
                i = i + same * pair_i[m]
            eps_a = virt[domain[i, a // VB]]
            turned[...] = jnp.broadcast_to(eps_a, (VB, VB)).T
            offset = pl.multiple_of(row % VB, piece)
            column = turned[pl.ds(offset, piece), :]
            for h in range(blocks):
                lanes = slice(h * VB, (h + 1) * VB)
                eps_b = virt[domain[j, v * blocks + h]]
                denominator = (column + eps_b) - occ_energy[i] - occ_energy[j]
                total = (
                    sums[pl.ds(row, piece), lanes]
                    + came[0, H - 1, pl.ds(local, piece), lanes].astype(F32)
                    + came[1, H - 1, pl.ds(local, piece), lanes].astype(F32)
                )
                amp[pl.ds(row, piece), lanes] = (-(total / denominator)).astype(BF16)

    for sub in (1, 0):
        amplitude(sub)
        ag_copy(0, 0, sub).start()
        ag_copy(1, 0, sub).start()

    def ag_body(t):
        for sub in (1, 0):
            for d in (0, 1):
                ag_copy(d, t - 1, sub).wait_recv()
                ag_copy(d, t, sub).start()

    steps(1, H - 1, ag_body)
    for d, sub in ((1, 1), (0, 0)):
        ag_copy(d, H - 2, sub).wait_recv()
        ag_copy(d, H - 1, sub).start()
    ag_copy(0, H - 2, 1).wait_recv()
    ag_copy(1, H - 2, 0).wait_recv()
    ag_copy(0, H - 1, 0).wait_recv()
    ag_copy(1, H - 1, 1).wait_recv()

    def mul(a, b):
        return jnp.dot(a, b, preferred_element_type=F32)

    def half_of(k, side):
        return amp[pl.ds(pl.multiple_of(k * width + side * half_width, half_width), half_width), :]

    def pair_product(k):
        i = pair_i[k]
        return mul(own[i], half_of(k, v)) + mul(peer[i], half_of(k, 1 - v))

    for e in range(extras):
        second[e] = pair_product(nocc + e)
    for j in range(nocc):
        value = pair_product(j)
        for e in range(extras):
            value = value + second[e] * holds(j, e).astype(F32)
        out[j] = value.astype(BF16)

    rs_copy(0, 0, 0).wait_send()
    rs_copy(1, 0, 1).wait_send()

    def rs_end(t):
        for d in (0, 1):
            for sub in (0, 1):
                rs_copy(d, t, sub).wait_send()

    steps(1, H, rs_end)

    def ag_end(t):
        for d in (0, 1):
            for sub in (0, 1):
                ag_copy(d, t, sub).wait_send()

    steps(0, H - 1, ag_end)
    ag_copy(0, H - 1, 0).wait_send()
    ag_copy(1, H - 1, 1).wait_send()


def on_device(integrals, virt_energy, occ_energy, domain, partners, pair_count):
    aux_count = lax.axis_size("aux")
    occ_count = lax.axis_size("occ")
    aux_rows, nocc, half_width = integrals.shape
    slot_count = partners.shape[1]
    pair_total = nocc * slot_count * 5 // 8
    width = half_width * lax.axis_size("vir")
    N = aux_count * occ_count
    H = N // 2
    rows = pair_total * width // N
    smem = pl.BlockSpec(memory_space=pltpu.SMEM)
    vmem = pl.BlockSpec(memory_space=pltpu.VMEM)
    gamma = pl.pallas_call(
        functools.partial(kernel, aux_count, occ_count, pair_total),
        out_shape=jax.ShapeDtypeStruct((nocc, aux_rows, half_width), BF16),
        in_specs=[smem] * 4 + [vmem] * 2,
        out_specs=vmem,
        scratch_shapes=[
            pltpu.VMEM((nocc, aux_rows, half_width), BF16),
            pltpu.VMEM((pair_total * width, half_width), F32),
            pltpu.VMEM((pair_total * width, half_width), BF16),
            pltpu.VMEM((2, H, rows, half_width), BF16),
            pltpu.VMEM((2, H, rows, half_width), BF16),
            pltpu.VMEM((VB, VB), F32),
            pltpu.VMEM((pair_total - nocc, aux_rows, half_width), F32),
            pltpu.SemaphoreType.DMA((2,)),
            pltpu.SemaphoreType.DMA((2, H, 2)),
            pltpu.SemaphoreType.DMA((2, H, 2)),
            pltpu.SemaphoreType.DMA((2, H, 2)),
            pltpu.SemaphoreType.DMA((2, H, 2)),
        ],
        compiler_params=pltpu.CompilerParams(
            collective_id=0, has_side_effects=True, vmem_limit_bytes=56 * 1024 * 1024
        ),
    )(
        partners, domain, pair_count, occ_energy,
        virt_energy.reshape(-1, 1, VB), jnp.transpose(integrals, (1, 0, 2)),
    )
    return jnp.transpose(gamma, (1, 0, 2))


def solution(mesh):
    in_specs = (
        P(("aux", "occ"), "groups", "vir"),
        P(),
        P("groups"),
        P("groups", None),
        P("groups", None),
        P("groups"),
    )
    out_specs = P(("aux", "occ"), "groups", "vir")
    return jax.shard_map(
        on_device, mesh=mesh, in_specs=in_specs, out_specs=out_specs, check_vma=False
    )
```

```python
import functools
import math

import jax
import jax.numpy as jnp
from jax import lax
from jax.experimental import pallas as pl
from jax.experimental.pallas import tpu as pltpu
from jax.sharding import PartitionSpec as P

VB = 128
MESH = pl.DeviceIdType.MESH
BF16 = jnp.bfloat16
F32 = jnp.float32


def grid_of(aux_count, occ_count):
    if occ_count == 1:
        return aux_count // 2, 2
    return aux_count, occ_count


def ring_place(z, x, Z, X):
    comb = x * (Z - 1) + jnp.where(x % 2 == 0, z - 1, Z - 1 - z)
    return jnp.where(z == 0, X * (Z - 1) + X - 1 - x, comb)


def ring_point(p, Z, X):
    x = p // (Z - 1)
    r = p % (Z - 1)
    comb_z = jnp.where(x % 2 == 0, r + 1, Z - 1 - r)
    back = p >= X * (Z - 1)
    return jnp.where(back, 0, comb_z), jnp.where(back, X - 1 - (p - X * (Z - 1)), x)


SUBS = 4
FIRST = ((0, 1), (2, 3))
RS_ORDER = ((2, 3, 0, 1), (0, 1, 2, 3))
AG_ORDER = (0, 2, 1, 3)


def cut(rows):
    units = rows // 16
    ends = [-(-units * (n + 1) // SUBS) * 16 for n in range(SUBS)]
    starts = [0] + ends[:-1]
    return tuple(e - b for b, e in zip(starts, ends)), tuple(starts)


def steps(low, high, body):
    if high - low <= 6:
        for t in range(low, high):
            body(t)
    elif high > low:
        lax.fori_loop(low, high, lambda t, c: (body(t), c)[1], 0)


def kernel(
    aux_count, occ_count, pair_total,
    partners, domain, count, occ_energy, virt, own,
    out,
    peer, sums, amp, sent, came, turned, scale, second,
    peer_sem, rs_send, rs_recv, ag_send, ag_recv,
):
    nocc, aux_rows, half_width = own.shape
    width = 2 * half_width
    Z, X = grid_of(aux_count, occ_count)
    N = Z * X
    H = N // 2
    rows = pair_total * width // N
    sub_rows, sub_off = cut(rows)
    group, aux, occ, v = (lax.axis_index(a) for a in ("groups", "aux", "occ", "vir"))
    if occ_count == 1:
        z, x = aux // X, aux % X
    else:
        z, x = aux, occ
    p = ring_place(z, x, Z, X)

    def device(q):
        qz, qx = ring_point(lax.rem(q + N, N), Z, X)
        if occ_count == 1:
            return (group, qz * X + qx, 0, v)
        return (group, qz, qx, v)

    target = (device(p + 1), device(p - 1))
    other = (group, aux, occ, 1 - v)
    barrier = pltpu.get_barrier_semaphore()
    for d in (*target, other):
        pl.semaphore_signal(barrier, inc=1, device_id=d, device_id_type=MESH)
    pl.semaphore_wait(barrier, 3)

    swap = pltpu.make_async_remote_copy(
        src_ref=own, dst_ref=peer, send_sem=peer_sem.at[0], recv_sem=peer_sem.at[1],
        device_id=other, device_id_type=MESH,
    )
    swap.start()

    ahead = []
    running = jnp.int32(0)
    for j in range(nocc):
        ahead.append(running)
        running = running + count[j] - 1
    def holds(j, e):
        apart = ahead[j] - e
        return (count[j] - 1) * jnp.maximum(1 - jnp.maximum(apart, -apart), 0)

    extras = pair_total - nocc
    pair_j = [jnp.int32(j) for j in range(nocc)]
    pair_i = [partners[0, j] for j in range(nocc)]
    for e in range(extras):
        pair_j.append(sum(holds(j, e) * j for j in range(nocc)))
        pair_i.append(sum(holds(j, e) * partners[1, j] for j in range(nocc)))

    def mul_t(a, b):
        return lax.dot_general(a, b, (((0,), (0,)), ((), ())), preferred_element_type=F32)

    for k in range(pair_total):
        at = pl.multiple_of(k * width + v * half_width, half_width)
        sums[pl.ds(at, half_width), :] = mul_t(own[pair_i[k]], own[pair_j[k]])
    swap.wait()
    for k in range(pair_total):
        at = pl.multiple_of(k * width + (1 - v) * half_width, half_width)
        sums[pl.ds(at, half_width), :] = mul_t(peer[pair_i[k]], own[pair_j[k]])

    def chunk_rows(c, sub):
        c = lax.rem(c + 2 * N, N)
        return pl.ds(pl.multiple_of(c * rows + sub_off[sub], 16), sub_rows[sub])

    def part(sub):
        return pl.ds(sub_off[sub], sub_rows[sub])

    def rs_copy(d, t, sub):
        return pltpu.make_async_remote_copy(
            src_ref=sent.at[d, t, part(sub), :], dst_ref=came.at[d, t, part(sub), :],
            send_sem=rs_send.at[d, t, sub], recv_sem=rs_recv.at[d, t, sub],
            device_id=target[d], device_id_type=MESH,
        )

    def rs_step(d, t, sub, add):
        sign = 1 - 2 * d
        value = sums[chunk_rows(p + sign * (H - t), sub), :]
        if add:
            rs_copy(d, t - 1, sub).wait_recv()
            value = value + came[d, t - 1, part(sub), :].astype(F32)
        sent[d, t, part(sub), :] = value.astype(BF16)
        rs_copy(d, t, sub).start()

    for n in range(SUBS // 2):
        for d in (0, 1):
            rs_step(d, 0, FIRST[d][n], False)
    for n in range(SUBS // 2):
        for d in (0, 1):
            rs_step(d, 1, RS_ORDER[d][n], False)

    piece = math.gcd(rows, VB)
    blocks = half_width // VB
    for q in range(rows // piece):
        row = pl.multiple_of(p * rows + q * piece, piece)
        k = row // width
        a = row % width
        j = jnp.int32(0)
        i = jnp.int32(0)
        for m in range(pair_total):
            same = (k == m).astype(jnp.int32)
            j = j + same * pair_j[m]
            i = i + same * pair_i[m]
        eps_a = virt[domain[a // VB, i]]
        turned[...] = jnp.broadcast_to(eps_a, (VB, VB)).T
        column = turned[pl.ds(pl.multiple_of(row % VB, piece), piece), :]
        for h in range(blocks):
            eps_b = virt[domain[v * blocks + h, j]]
            denominator = (column + eps_b) - occ_energy[i] - occ_energy[j]
            scale[pl.ds(q * piece, piece), slice(h * VB, (h + 1) * VB)] = -1.0 / denominator

    for n in range(SUBS // 2, SUBS):
        for d in (0, 1):
            rs_step(d, 1, RS_ORDER[d][n], True)

    def rs_body(t):
        for n in range(SUBS):
            for d in (0, 1):
                rs_step(d, t, RS_ORDER[d][n], True)

    steps(2, H, rs_body)

    def ag_copy(d, t, sub):
        where = chunk_rows(p - (1 - 2 * d) * t, sub)
        return pltpu.make_async_remote_copy(
            src_ref=amp.at[where, :], dst_ref=amp.at[where, :],
            send_sem=ag_send.at[d, t, sub], recv_sem=ag_recv.at[d, t, sub],
            device_id=target[d], device_id_type=MESH,
        )

    for sub in AG_ORDER:
        for d in (0, 1):
            rs_copy(d, H - 1, sub).wait_recv()
        total = (
            sums[chunk_rows(p, sub), :]
            + came[0, H - 1, part(sub), :].astype(F32)
            + came[1, H - 1, part(sub), :].astype(F32)
        )
        amp[chunk_rows(p, sub), :] = (total * scale[part(sub), :]).astype(BF16)
        for d in (0, 1):
            ag_copy(d, 0, sub).start()

    def ag_body(t):
        for sub in AG_ORDER:
            for d in (0, 1):
                ag_copy(d, t - 1, sub).wait_recv()
                ag_copy(d, t, sub).start()

    steps(1, H - 1, ag_body)
    for sub in AG_ORDER:
        for d in (0, 1):
            ag_copy(d, H - 2, sub).wait_recv()
            if sub in FIRST[d]:
                ag_copy(d, H - 1, sub).start()
    for d in (0, 1):
        for sub in FIRST[d]:
            ag_copy(d, H - 1, sub).wait_recv()

    def mul(a, b):
        return jnp.dot(a, b, preferred_element_type=F32)

    def half_of(k, side):
        return amp[pl.ds(pl.multiple_of(k * width + side * half_width, half_width), half_width), :]

    def pair_product(k):
        i = pair_i[k]
        return mul(own[i], half_of(k, v)) + mul(peer[i], half_of(k, 1 - v))

    for e in range(extras):
        second[e] = pair_product(nocc + e)
    for j in range(nocc):
        value = pair_product(j)
        for e in range(extras):
            value = value + second[e] * holds(j, e).astype(F32)
        out[j] = value.astype(BF16)

    for d in (0, 1):
        for sub in FIRST[d]:
            rs_copy(d, 0, sub).wait_send()
            ag_copy(d, H - 1, sub).wait_send()

    def end(t):
        for d in (0, 1):
            for sub in range(SUBS):
                rs_copy(d, t + 1, sub).wait_send()
                ag_copy(d, t, sub).wait_send()

    steps(0, H - 1, end)


def on_device(integrals, virt_energy, occ_energy, domain, partners, pair_count):
    aux_count = lax.axis_size("aux")
    occ_count = lax.axis_size("occ")
    aux_rows, nocc, half_width = integrals.shape
    slot_count = partners.shape[1]
    pair_total = nocc * slot_count * 5 // 8
    width = half_width * lax.axis_size("vir")
    N = aux_count * occ_count
    H = N // 2
    rows = pair_total * width // N
    smem = pl.BlockSpec(memory_space=pltpu.SMEM)
    vmem = pl.BlockSpec(memory_space=pltpu.VMEM)
    gamma = pl.pallas_call(
        functools.partial(kernel, aux_count, occ_count, pair_total),
        out_shape=jax.ShapeDtypeStruct((nocc, aux_rows, half_width), BF16),
        in_specs=[smem] * 4 + [vmem] * 2,
        out_specs=vmem,
        scratch_shapes=[
            pltpu.VMEM((nocc, aux_rows, half_width), BF16),
            pltpu.VMEM((pair_total * width, half_width), F32),
            pltpu.VMEM((pair_total * width, half_width), BF16),
            pltpu.VMEM((2, H, rows, half_width), BF16),
            pltpu.VMEM((2, H, rows, half_width), BF16),
            pltpu.VMEM((VB, VB), F32),
            pltpu.VMEM((rows, half_width), F32),
            pltpu.VMEM((pair_total - nocc, aux_rows, half_width), F32),
            pltpu.SemaphoreType.DMA((2,)),
            pltpu.SemaphoreType.DMA((2, H, SUBS)),
            pltpu.SemaphoreType.DMA((2, H, SUBS)),
            pltpu.SemaphoreType.DMA((2, H, SUBS)),
            pltpu.SemaphoreType.DMA((2, H, SUBS)),
        ],
        compiler_params=pltpu.CompilerParams(
            collective_id=0, has_side_effects=True, vmem_limit_bytes=56 * 1024 * 1024
        ),
    )(
        partners.T, domain.T, pair_count, occ_energy,
        virt_energy.reshape(-1, 1, VB), jnp.transpose(integrals, (1, 0, 2)),
    )
    return jnp.transpose(gamma, (1, 0, 2))


def solution(mesh):
    in_specs = (
        P(("aux", "occ"), "groups", "vir"),
        P(),
        P("groups"),
        P("groups", None),
        P("groups", None),
        P("groups"),
    )
    out_specs = P(("aux", "occ"), "groups", "vir")
    return jax.shard_map(
        on_device, mesh=mesh, in_specs=in_specs, out_specs=out_specs, check_vma=False
    )
```

```python
import functools
import math

import jax
import jax.numpy as jnp
from jax import lax
from jax.experimental import pallas as pl
from jax.experimental.pallas import tpu as pltpu
from jax.sharding import PartitionSpec as P

VB = 128
MESH = pl.DeviceIdType.MESH
BF16 = jnp.bfloat16
F32 = jnp.float32


def grid_of(aux_count, occ_count):
    if occ_count == 1:
        return aux_count // 2, 2
    return aux_count, occ_count


def ring_place(z, x, Z, X):
    comb = x * (Z - 1) + jnp.where(x % 2 == 0, z - 1, Z - 1 - z)
    return jnp.where(z == 0, X * (Z - 1) + X - 1 - x, comb)


def ring_point(p, Z, X):
    x = p // (Z - 1)
    r = p % (Z - 1)
    comb_z = jnp.where(x % 2 == 0, r + 1, Z - 1 - r)
    back = p >= X * (Z - 1)
    return jnp.where(back, 0, comb_z), jnp.where(back, X - 1 - (p - X * (Z - 1)), x)


SUBS = 4
FIRST = ((0, 1), (2, 3))
RS_ORDER = ((2, 3, 0, 1), (0, 1, 2, 3))
AG_ORDER = (0, 2, 1, 3)


def cut(rows):
    units = rows // 16
    ends = [-(-units * (n + 1) // SUBS) * 16 for n in range(SUBS)]
    starts = [0] + ends[:-1]
    return tuple(e - b for b, e in zip(starts, ends)), tuple(starts)


def steps(low, high, body):
    if high - low <= 6:
        for t in range(low, high):
            body(t)
    elif high > low:
        lax.fori_loop(low, high, lambda t, c: (body(t), c)[1], 0)


def kernel(
    aux_count, occ_count, pair_total,
    partners, domain, count, occ_energy, virt, own,
    out,
    peer, sums, amp, sent, came, turned, scale, second,
    peer_sem, rs_send, rs_recv, ag_send, ag_recv,
):
    nocc, aux_rows, half_width = own.shape
    width = 2 * half_width
    Z, X = grid_of(aux_count, occ_count)
    N = Z * X
    H = N // 2
    rows = pair_total * width // N
    sub_rows, sub_off = cut(rows)
    group, aux, occ, v = (lax.axis_index(a) for a in ("groups", "aux", "occ", "vir"))
    if occ_count == 1:
        z, x = aux // X, aux % X
    else:
        z, x = aux, occ
    p = ring_place(z, x, Z, X)

    def device(q):
        qz, qx = ring_point(lax.rem(q + N, N), Z, X)
        if occ_count == 1:
            return (group, qz * X + qx, 0, v)
        return (group, qz, qx, v)

    target = (device(p + 1), device(p - 1))
    other = (group, aux, occ, 1 - v)
    barrier = pltpu.get_barrier_semaphore()
    for d in (*target, other):
        pl.semaphore_signal(barrier, inc=1, device_id=d, device_id_type=MESH)
    pl.semaphore_wait(barrier, 3)

    swap = pltpu.make_async_remote_copy(
        src_ref=own, dst_ref=peer, send_sem=peer_sem.at[0], recv_sem=peer_sem.at[1],
        device_id=other, device_id_type=MESH,
    )
    swap.start()

    ahead = []
    running = jnp.int32(0)
    for j in range(nocc):
        ahead.append(running)
        running = running + count[j] - 1
    def holds(j, e):
        apart = ahead[j] - e
        return (count[j] - 1) * jnp.maximum(1 - jnp.maximum(apart, -apart), 0)

    extras = pair_total - nocc
    pair_j = [jnp.int32(j) for j in range(nocc)]
    pair_i = [partners[0, j] for j in range(nocc)]
    for e in range(extras):
        pair_j.append(sum(holds(j, e) * j for j in range(nocc)))
        pair_i.append(sum(holds(j, e) * partners[1, j] for j in range(nocc)))

    def mul_t(a, b):
        return lax.dot_general(a, b, (((0,), (0,)), ((), ())), preferred_element_type=F32)

    split = rows % 64 == 0
    half_rows = rows // 2

    def half_at(k, far):
        if split:
            return pl.ds((far * pair_total + k) * half_width, half_width)
        side = 1 - v if far else v
        return pl.ds(pl.multiple_of(k * width + side * half_width, half_width), half_width)

    def chunk_rows(c, sub):
        c = lax.rem(c + 2 * N, N)
        if split:
            far = sub_off[sub] // half_rows
            start = far * pair_total * half_width + c * half_rows + sub_off[sub] - far * half_rows
        else:
            start = c * rows + sub_off[sub]
        return pl.ds(pl.multiple_of(start, 16), sub_rows[sub])

    def pair_sums(source, far):
        for k in range(pair_total):
            sums[half_at(k, far), :] = mul_t(source[pair_i[k]], own[pair_j[k]])

    pair_sums(own, 0)
    if not split:
        swap.wait()
        pair_sums(peer, 1)

    def part(sub):
        return pl.ds(sub_off[sub], sub_rows[sub])

    def rs_copy(d, t, sub):
        return pltpu.make_async_remote_copy(
            src_ref=sent.at[d, t, part(sub), :], dst_ref=came.at[d, t, part(sub), :],
            send_sem=rs_send.at[d, t, sub], recv_sem=rs_recv.at[d, t, sub],
            device_id=target[d], device_id_type=MESH,
        )

    def rs_step(d, t, sub, add):
        sign = 1 - 2 * d
        value = sums[chunk_rows(p + sign * (H - t), sub), :]
        if add:
            rs_copy(d, t - 1, sub).wait_recv()
            value = value + came[d, t - 1, part(sub), :].astype(F32)
        sent[d, t, part(sub), :] = value.astype(BF16)
        rs_copy(d, t, sub).start()

    for sub in (0, 1):
        for d in (0, 1):
            rs_step(d, d, sub, False)
    if split:
        swap.wait()
        pair_sums(peer, 1)
    for sub in (2, 3):
        for d in (0, 1):
            rs_step(d, 1 - d, sub, False)

    piece = math.gcd(half_rows if split else rows, VB)
    blocks = half_width // VB
    for q in range(rows // piece):
        if split:
            far = q * piece // half_rows
            row = p * half_rows + q * piece - far * half_rows
            k = row // half_width
            a = row % half_width + (1 - v if far else v) * half_width
        else:
            row = p * rows + q * piece
            k = row // width
            a = row % width
        j = jnp.int32(0)
        i = jnp.int32(0)
        for m in range(pair_total):
            same = (k == m).astype(jnp.int32)
            j = j + same * pair_j[m]
            i = i + same * pair_i[m]
        eps_a = virt[domain[a // VB, i]]
        turned[...] = jnp.broadcast_to(eps_a, (VB, VB)).T
        column = turned[pl.ds(pl.multiple_of(a % VB, piece), piece), :]
        for h in range(blocks):
            eps_b = virt[domain[v * blocks + h, j]]
            denominator = (column + eps_b) - occ_energy[i] - occ_energy[j]
            scale[pl.ds(q * piece, piece), slice(h * VB, (h + 1) * VB)] = -1.0 / denominator

    for n in range(SUBS // 2, SUBS):
        for d in (0, 1):
            rs_step(d, 1, RS_ORDER[d][n], True)

    def rs_body(t):
        for n in range(SUBS):
            for d in (0, 1):
                rs_step(d, t, RS_ORDER[d][n], True)

    steps(2, H, rs_body)

    def ag_copy(d, t, sub):
        where = chunk_rows(p - (1 - 2 * d) * t, sub)
        return pltpu.make_async_remote_copy(
            src_ref=amp.at[where, :], dst_ref=amp.at[where, :],
            send_sem=ag_send.at[d, t, sub], recv_sem=ag_recv.at[d, t, sub],
            device_id=target[d], device_id_type=MESH,
        )

    for sub in AG_ORDER:
        for d in (0, 1):
            rs_copy(d, H - 1, sub).wait_recv()
        total = (
            sums[chunk_rows(p, sub), :]
            + came[0, H - 1, part(sub), :].astype(F32)
            + came[1, H - 1, part(sub), :].astype(F32)
        )
        amp[chunk_rows(p, sub), :] = (total * scale[part(sub), :]).astype(BF16)
        for d in (0, 1):
            ag_copy(d, 0, sub).start()

    def ag_body(t):
        for sub in AG_ORDER:
            for d in (0, 1):
                ag_copy(d, t - 1, sub).wait_recv()
                ag_copy(d, t, sub).start()

    steps(1, H - 1, ag_body)
    for sub in AG_ORDER:
        for d in (0, 1):
            ag_copy(d, H - 2, sub).wait_recv()
            if sub in FIRST[d]:
                ag_copy(d, H - 1, sub).start()
    for d in (0, 1):
        for sub in FIRST[d]:
            ag_copy(d, H - 1, sub).wait_recv()

    def mul(a, b):
        return jnp.dot(a, b, preferred_element_type=F32)

    def pair_product(k):
        i = pair_i[k]
        return mul(own[i], amp[half_at(k, 0), :]) + mul(peer[i], amp[half_at(k, 1), :])

    for e in range(extras):
        second[e] = pair_product(nocc + e)
    for j in range(nocc):
        value = pair_product(j)
        for e in range(extras):
            value = value + second[e] * holds(j, e).astype(F32)
        out[j] = value.astype(BF16)

    for d in (0, 1):
        for sub in FIRST[d]:
            rs_copy(d, 0, sub).wait_send()
            ag_copy(d, H - 1, sub).wait_send()

    def end(t):
        for d in (0, 1):
            for sub in range(SUBS):
                rs_copy(d, t + 1, sub).wait_send()
                ag_copy(d, t, sub).wait_send()

    steps(0, H - 1, end)


def on_device(integrals, virt_energy, occ_energy, domain, partners, pair_count):
    aux_count = lax.axis_size("aux")
    occ_count = lax.axis_size("occ")
    aux_rows, nocc, half_width = integrals.shape
    slot_count = partners.shape[1]
    pair_total = nocc * slot_count * 5 // 8
    width = half_width * lax.axis_size("vir")
    N = aux_count * occ_count
    H = N // 2
    rows = pair_total * width // N
    smem = pl.BlockSpec(memory_space=pltpu.SMEM)
    vmem = pl.BlockSpec(memory_space=pltpu.VMEM)
    gamma = pl.pallas_call(
        functools.partial(kernel, aux_count, occ_count, pair_total),
        out_shape=jax.ShapeDtypeStruct((nocc, aux_rows, half_width), BF16),
        in_specs=[smem] * 4 + [vmem] * 2,
        out_specs=vmem,
        scratch_shapes=[
            pltpu.VMEM((nocc, aux_rows, half_width), BF16),
            pltpu.VMEM((pair_total * width, half_width), F32),
            pltpu.VMEM((pair_total * width, half_width), BF16),
            pltpu.VMEM((2, H, rows, half_width), BF16),
            pltpu.VMEM((2, H, rows, half_width), BF16),
            pltpu.VMEM((VB, VB), F32),
            pltpu.VMEM((rows, half_width), F32),
            pltpu.VMEM((pair_total - nocc, aux_rows, half_width), F32),
            pltpu.SemaphoreType.DMA((2,)),
            pltpu.SemaphoreType.DMA((2, H, SUBS)),
            pltpu.SemaphoreType.DMA((2, H, SUBS)),
            pltpu.SemaphoreType.DMA((2, H, SUBS)),
            pltpu.SemaphoreType.DMA((2, H, SUBS)),
        ],
        compiler_params=pltpu.CompilerParams(
            collective_id=0, has_side_effects=True, vmem_limit_bytes=56 * 1024 * 1024
        ),
    )(
        partners.T, domain.T, pair_count, occ_energy,
        virt_energy.reshape(-1, 1, VB), jnp.transpose(integrals, (1, 0, 2)),
    )
    return jnp.transpose(gamma, (1, 0, 2))


def solution(mesh):
    in_specs = (
        P(("aux", "occ"), "groups", "vir"),
        P(),
        P("groups"),
        P("groups", None),
        P("groups", None),
        P("groups"),
    )
    out_specs = P(("aux", "occ"), "groups", "vir")
    return jax.shard_map(
        on_device, mesh=mesh, in_specs=in_specs, out_specs=out_specs, check_vma=False
    )
```

```python
import functools
import math

import jax
import jax.numpy as jnp
from jax import lax
from jax.experimental import pallas as pl
from jax.experimental.pallas import tpu as pltpu
from jax.sharding import PartitionSpec as P

VB = 128
MESH = pl.DeviceIdType.MESH
BF16 = jnp.bfloat16
F32 = jnp.float32


def grid_of(aux_count, occ_count):
    if occ_count == 1:
        return aux_count // 2, 2
    return aux_count, occ_count


def ring_place(z, x, Z, X):
    comb = x * (Z - 1) + jnp.where(x % 2 == 0, z - 1, Z - 1 - z)
    return jnp.where(z == 0, X * (Z - 1) + X - 1 - x, comb)


def ring_point(p, Z, X):
    x = p // (Z - 1)
    r = p % (Z - 1)
    comb_z = jnp.where(x % 2 == 0, r + 1, Z - 1 - r)
    back = p >= X * (Z - 1)
    return jnp.where(back, 0, comb_z), jnp.where(back, X - 1 - (p - X * (Z - 1)), x)


SUBS = 4
FIRST = ((0, 1), (2, 3))
RS_ORDER = ((2, 3, 0, 1), (0, 1, 2, 3))
AG_ORDER = (0, 2, 1, 3)


def cut(rows):
    units = rows // 16
    ends = [-(-units * (n + 1) // SUBS) * 16 for n in range(SUBS)]
    starts = [0] + ends[:-1]
    return tuple(e - b for b, e in zip(starts, ends)), tuple(starts)


def steps(low, high, body):
    if high - low <= 6:
        for t in range(low, high):
            body(t)
    elif high > low:
        lax.fori_loop(low, high, lambda t, c: (body(t), c)[1], 0)


def kernel(
    aux_count, occ_count, pair_total,
    partners, domain, count, occ_energy, virt, own,
    out,
    peer, sums, amp, sent, came, turned, scale, products,
    peer_sem, rs_send, rs_recv, ag_send, ag_recv,
):
    nocc, aux_rows, half_width = own.shape
    width = 2 * half_width
    Z, X = grid_of(aux_count, occ_count)
    N = Z * X
    H = N // 2
    rows = pair_total * width // N
    sub_rows, sub_off = cut(rows)
    group, aux, occ, v = (lax.axis_index(a) for a in ("groups", "aux", "occ", "vir"))
    if occ_count == 1:
        z, x = aux // X, aux % X
    else:
        z, x = aux, occ
    p = ring_place(z, x, Z, X)

    def device(q):
        qz, qx = ring_point(lax.rem(q + N, N), Z, X)
        if occ_count == 1:
            return (group, qz * X + qx, 0, v)
        return (group, qz, qx, v)

    target = (device(p + 1), device(p - 1))
    other = (group, aux, occ, 1 - v)
    barrier = pltpu.get_barrier_semaphore()
    for d in (*target, other):
        pl.semaphore_signal(barrier, inc=1, device_id=d, device_id_type=MESH)
    pl.semaphore_wait(barrier, 3)

    swap = pltpu.make_async_remote_copy(
        src_ref=own, dst_ref=peer, send_sem=peer_sem.at[0], recv_sem=peer_sem.at[1],
        device_id=other, device_id_type=MESH,
    )
    swap.start()

    ahead = []
    running = jnp.int32(0)
    for j in range(nocc):
        ahead.append(running)
        running = running + count[j] - 1
    def holds(j, e):
        apart = ahead[j] - e
        return (count[j] - 1) * jnp.maximum(1 - jnp.maximum(apart, -apart), 0)

    extras = pair_total - nocc
    pair_j = [jnp.int32(j) for j in range(nocc)]
    pair_i = [partners[0, j] for j in range(nocc)]
    for e in range(extras):
        pair_j.append(sum(holds(j, e) * j for j in range(nocc)))
        pair_i.append(sum(holds(j, e) * partners[1, j] for j in range(nocc)))

    def mul_t(a, b):
        return lax.dot_general(a, b, (((0,), (0,)), ((), ())), preferred_element_type=F32)

    split = rows % 64 == 0
    half_rows = rows // 2

    def half_at(k, far):
        if split:
            return pl.ds(pl.multiple_of((far * pair_total + k) * half_width, half_width), half_width)
        side = 1 - v if far else v
        return pl.ds(pl.multiple_of(k * width + side * half_width, half_width), half_width)

    def chunk_rows(c, sub):
        c = lax.rem(c + 2 * N, N)
        if split:
            far = sub_off[sub] // half_rows
            start = far * pair_total * half_width + c * half_rows + sub_off[sub] - far * half_rows
        else:
            start = c * rows + sub_off[sub]
        return pl.ds(pl.multiple_of(start, 16), sub_rows[sub])

    def pair_sums(source, far):
        for k in range(pair_total):
            sums[half_at(k, far), :] = mul_t(source[pair_i[k]], own[pair_j[k]])

    pair_sums(own, 0)
    if not split:
        swap.wait()
        pair_sums(peer, 1)

    def part(sub):
        return pl.ds(sub_off[sub], sub_rows[sub])

    def rs_copy(d, t, sub):
        return pltpu.make_async_remote_copy(
            src_ref=sent.at[d, t, part(sub), :], dst_ref=came.at[d, t, part(sub), :],
            send_sem=rs_send.at[d, t, sub], recv_sem=rs_recv.at[d, t, sub],
            device_id=target[d], device_id_type=MESH,
        )

    def rs_step(d, t, sub, add):
        sign = 1 - 2 * d
        value = sums[chunk_rows(p + sign * (H - t), sub), :]
        if add:
            rs_copy(d, t - 1, sub).wait_recv()
            value = value + came[d, t - 1, part(sub), :].astype(F32)
        sent[d, t, part(sub), :] = value.astype(BF16)
        rs_copy(d, t, sub).start()

    for sub in (0, 1):
        for d in (0, 1):
            rs_step(d, d, sub, False)
    if split:
        swap.wait()
        pair_sums(peer, 1)
    for sub in (2, 3):
        for d in (0, 1):
            rs_step(d, 1 - d, sub, False)

    piece = math.gcd(half_rows if split else rows, VB)
    blocks = half_width // VB
    for q in range(rows // piece):
        if split:
            far = q * piece // half_rows
            row = p * half_rows + q * piece - far * half_rows
            k = row // half_width
            a = row % half_width + (1 - v if far else v) * half_width
        else:
            row = p * rows + q * piece
            k = row // width
            a = row % width
        j = jnp.int32(0)
        i = jnp.int32(0)
        for m in range(pair_total):
            same = (k == m).astype(jnp.int32)
            j = j + same * pair_j[m]
            i = i + same * pair_i[m]
        eps_a = virt[domain[a // VB, i]]
        turned[...] = jnp.broadcast_to(eps_a, (VB, VB)).T
        column = turned[pl.ds(pl.multiple_of(a % VB, piece), piece), :]
        for h in range(blocks):
            eps_b = virt[domain[v * blocks + h, j]]
            denominator = (column + eps_b) - occ_energy[i] - occ_energy[j]
            scale[pl.ds(q * piece, piece), slice(h * VB, (h + 1) * VB)] = -1.0 / denominator

    for n in range(SUBS // 2, SUBS):
        for d in (0, 1):
            rs_step(d, 1, RS_ORDER[d][n], True)

    def rs_body(t):
        for n in range(SUBS):
            for d in (0, 1):
                rs_step(d, t, RS_ORDER[d][n], True)

    steps(2, H, rs_body)

    def ag_copy(d, t, sub):
        where = chunk_rows(p - (1 - 2 * d) * t, sub)
        return pltpu.make_async_remote_copy(
            src_ref=amp.at[where, :], dst_ref=amp.at[where, :],
            send_sem=ag_send.at[d, t, sub], recv_sem=ag_recv.at[d, t, sub],
            device_id=target[d], device_id_type=MESH,
        )

    for sub in AG_ORDER:
        for d in (0, 1):
            rs_copy(d, H - 1, sub).wait_recv()
        total = (
            sums[chunk_rows(p, sub), :]
            + came[0, H - 1, part(sub), :].astype(F32)
            + came[1, H - 1, part(sub), :].astype(F32)
        )
        amp[chunk_rows(p, sub), :] = (total * scale[part(sub), :]).astype(BF16)
        for d in (0, 1):
            ag_copy(d, 0, sub).start()

    def ag_body(t):
        for sub in AG_ORDER:
            for d in (0, 1):
                ag_copy(d, t - 1, sub).wait_recv()
                ag_copy(d, t, sub).start()

    steps(1, H - 1, ag_body)
    for sub in AG_ORDER:
        for d in (0, 1):
            ag_copy(d, H - 2, sub).wait_recv()
            if sub in FIRST[d]:
                ag_copy(d, H - 1, sub).start()
    def mul(a, b):
        return jnp.dot(a, b, preferred_element_type=F32)

    def pair_product(k):
        i = jnp.int32(0)
        for m in range(pair_total):
            i = i + (k == m).astype(jnp.int32) * pair_i[m]
        return mul(own[i], amp[half_at(k, 0), :]) + mul(peer[i], amp[half_at(k, 1), :])

    late = pair_total
    start = 0
    if split:
        step = math.gcd(half_rows, half_width)
        late = (half_width - step + half_rows - 1) // half_width + 1
        start = lax.rem(p + H, N) * half_rows // half_width

    def do_pair(n):
        k = lax.rem(jnp.int32(start + n), pair_total)
        products[k] = pair_product(k)

    for n in range(late, pair_total):
        do_pair(n)
    for d in (0, 1):
        for sub in FIRST[d]:
            ag_copy(d, H - 1, sub).wait_recv()

    for n in range(late):
        do_pair(n)
    for j in range(nocc):
        value = products[j]
        for e in range(extras):
            value = value + products[nocc + e] * holds(j, e).astype(F32)
        out[j] = value.astype(BF16)

    for d in (0, 1):
        for sub in FIRST[d]:
            rs_copy(d, 0, sub).wait_send()
            ag_copy(d, H - 1, sub).wait_send()

    def end(t):
        for d in (0, 1):
            for sub in range(SUBS):
                rs_copy(d, t + 1, sub).wait_send()
                ag_copy(d, t, sub).wait_send()

    steps(0, H - 1, end)


def on_device(integrals, virt_energy, occ_energy, domain, partners, pair_count):
    aux_count = lax.axis_size("aux")
    occ_count = lax.axis_size("occ")
    aux_rows, nocc, half_width = integrals.shape
    slot_count = partners.shape[1]
    pair_total = nocc * slot_count * 5 // 8
    width = half_width * lax.axis_size("vir")
    N = aux_count * occ_count
    H = N // 2
    rows = pair_total * width // N
    smem = pl.BlockSpec(memory_space=pltpu.SMEM)
    vmem = pl.BlockSpec(memory_space=pltpu.VMEM)
    gamma = pl.pallas_call(
        functools.partial(kernel, aux_count, occ_count, pair_total),
        out_shape=jax.ShapeDtypeStruct((nocc, aux_rows, half_width), BF16),
        in_specs=[smem] * 4 + [vmem] * 2,
        out_specs=vmem,
        scratch_shapes=[
            pltpu.VMEM((nocc, aux_rows, half_width), BF16),
            pltpu.VMEM((pair_total * width, half_width), F32),
            pltpu.VMEM((pair_total * width, half_width), BF16),
            pltpu.VMEM((2, H, rows, half_width), BF16),
            pltpu.VMEM((2, H, rows, half_width), BF16),
            pltpu.VMEM((VB, VB), F32),
            pltpu.VMEM((rows, half_width), F32),
            pltpu.VMEM((pair_total, aux_rows, half_width), F32),
            pltpu.SemaphoreType.DMA((2,)),
            pltpu.SemaphoreType.DMA((2, H, SUBS)),
            pltpu.SemaphoreType.DMA((2, H, SUBS)),
            pltpu.SemaphoreType.DMA((2, H, SUBS)),
            pltpu.SemaphoreType.DMA((2, H, SUBS)),
        ],
        compiler_params=pltpu.CompilerParams(
            collective_id=0, has_side_effects=True, vmem_limit_bytes=56 * 1024 * 1024
        ),
    )(
        partners.T, domain.T, pair_count, occ_energy,
        virt_energy.reshape(-1, 1, VB), jnp.transpose(integrals, (1, 0, 2)),
    )
    return jnp.transpose(gamma, (1, 0, 2))


def solution(mesh):
    in_specs = (
        P(("aux", "occ"), "groups", "vir"),
        P(),
        P("groups"),
        P("groups", None),
        P("groups", None),
        P("groups"),
    )
    out_specs = P(("aux", "occ"), "groups", "vir")
    return jax.shard_map(
        on_device, mesh=mesh, in_specs=in_specs, out_specs=out_specs, check_vma=False
    )
```

```python
import functools
import math

import jax
import jax.numpy as jnp
from jax import lax
from jax.experimental import pallas as pl
from jax.experimental.pallas import tpu as pltpu
from jax.sharding import PartitionSpec as P

VB = 128
MESH = pl.DeviceIdType.MESH
BF16 = jnp.bfloat16
F32 = jnp.float32


def grid_of(aux_count, occ_count):
    if occ_count == 1:
        return aux_count // 2, 2
    return aux_count, occ_count


def ring_place(z, x, Z, X):
    comb = x * (Z - 1) + jnp.where(x % 2 == 0, z - 1, Z - 1 - z)
    return jnp.where(z == 0, X * (Z - 1) + X - 1 - x, comb)


def ring_point(p, Z, X):
    x = p // (Z - 1)
    r = p % (Z - 1)
    comb_z = jnp.where(x % 2 == 0, r + 1, Z - 1 - r)
    back = p >= X * (Z - 1)
    return jnp.where(back, 0, comb_z), jnp.where(back, X - 1 - (p - X * (Z - 1)), x)


SUBS = 4
FIRST = ((0, 1), (2, 3))
RS_ORDER = ((2, 3, 0, 1), (0, 1, 2, 3))
AG_ORDER = (0, 2, 1, 3)


def cut(rows):
    units = rows // 16
    ends = [-(-units * (n + 1) // SUBS) * 16 for n in range(SUBS)]
    starts = [0] + ends[:-1]
    return tuple(e - b for b, e in zip(starts, ends)), tuple(starts)


def steps(low, high, body):
    if high - low <= 6:
        for t in range(low, high):
            body(t)
    elif high > low:
        lax.fori_loop(low, high, lambda t, c: (body(t), c)[1], 0)


def kernel(
    aux_count, occ_count, pair_total,
    partners, domain, count, occ_energy, virt, own,
    out,
    peer, sums, amp, sent, came, turned, scale, products,
    peer_sem, rs_send, rs_recv, ag_send, ag_recv,
):
    nocc, aux_rows, half_width = own.shape
    width = 2 * half_width
    Z, X = grid_of(aux_count, occ_count)
    N = Z * X
    H = N // 2
    rows = pair_total * width // N
    sub_rows, sub_off = cut(rows)
    group, aux, occ, v = (lax.axis_index(a) for a in ("groups", "aux", "occ", "vir"))
    if occ_count == 1:
        z, x = aux // X, aux % X
    else:
        z, x = aux, occ
    p = ring_place(z, x, Z, X)

    def device(q):
        qz, qx = ring_point(lax.rem(q + N, N), Z, X)
        if occ_count == 1:
            return (group, qz * X + qx, 0, v)
        return (group, qz, qx, v)

    target = (device(p + 1), device(p - 1))
    other = (group, aux, occ, 1 - v)
    barrier = pltpu.get_barrier_semaphore()
    for d in (*target, other):
        pl.semaphore_signal(barrier, inc=1, device_id=d, device_id_type=MESH)
    pl.semaphore_wait(barrier, 3)

    swap = pltpu.make_async_remote_copy(
        src_ref=own, dst_ref=peer, send_sem=peer_sem.at[0], recv_sem=peer_sem.at[1],
        device_id=other, device_id_type=MESH,
    )
    swap.start()

    ahead = []
    running = jnp.int32(0)
    for j in range(nocc):
        ahead.append(running)
        running = running + count[j] - 1
    def holds(j, e):
        apart = ahead[j] - e
        return (count[j] - 1) * jnp.maximum(1 - jnp.maximum(apart, -apart), 0)

    extras = pair_total - nocc
    pair_j = [jnp.int32(j) for j in range(nocc)]
    pair_i = [partners[0, j] for j in range(nocc)]
    for e in range(extras):
        pair_j.append(sum(holds(j, e) * j for j in range(nocc)))
        pair_i.append(sum(holds(j, e) * partners[1, j] for j in range(nocc)))

    def mul_t(a, b):
        return lax.dot_general(a, b, (((0,), (0,)), ((), ())), preferred_element_type=F32)

    split = rows % 64 == 0
    half_rows = rows // 2

    def half_at(k, far):
        if split:
            return pl.ds(pl.multiple_of((far * pair_total + k) * half_width, half_width), half_width)
        side = 1 - v if far else v
        return pl.ds(pl.multiple_of(k * width + side * half_width, half_width), half_width)

    def chunk_rows(c, sub):
        c = lax.rem(c + 2 * N, N)
        if split:
            far = sub_off[sub] // half_rows
            start = far * pair_total * half_width + c * half_rows + sub_off[sub] - far * half_rows
        else:
            start = c * rows + sub_off[sub]
        return pl.ds(pl.multiple_of(start, 16), sub_rows[sub])

    def pair_sums(source, far):
        for k in range(pair_total):
            sums[half_at(k, far), :] = mul_t(source[pair_i[k]], own[pair_j[k]])

    pair_sums(own, 0)
    if not split:
        swap.wait()
        pair_sums(peer, 1)

    def part(sub):
        return pl.ds(sub_off[sub], sub_rows[sub])

    def rs_copy(d, t, sub):
        return pltpu.make_async_remote_copy(
            src_ref=sent.at[d, t, part(sub), :], dst_ref=came.at[d, t, part(sub), :],
            send_sem=rs_send.at[d, t, sub], recv_sem=rs_recv.at[d, t, sub],
            device_id=target[d], device_id_type=MESH,
        )

    def rs_step(d, t, sub, add):
        sign = 1 - 2 * d
        value = sums[chunk_rows(p + sign * (H - t), sub), :]
        if add:
            rs_copy(d, t - 1, sub).wait_recv()
            value = value + came[d, t - 1, part(sub), :].astype(F32)
        sent[d, t, part(sub), :] = value.astype(BF16)
        rs_copy(d, t, sub).start()

    for sub in (0, 1):
        for d in (0, 1):
            rs_step(d, d, sub, False)
    if split:
        swap.wait()
        pair_sums(peer, 1)
    for sub in (2, 3):
        for d in (0, 1):
            rs_step(d, 1 - d, sub, False)

    piece = math.gcd(half_rows if split else rows, VB)
    blocks = half_width // VB
    for q in range(rows // piece):
        if split:
            far = q * piece // half_rows
            row = p * half_rows + q * piece - far * half_rows
            k = row // half_width
            a = row % half_width + (1 - v if far else v) * half_width
        else:
            row = p * rows + q * piece
            k = row // width
            a = row % width
        j = jnp.int32(0)
        i = jnp.int32(0)
        for m in range(pair_total):
            same = (k == m).astype(jnp.int32)
            j = j + same * pair_j[m]
            i = i + same * pair_i[m]
        eps_a = virt[domain[a // VB, i]]
        turned[...] = jnp.broadcast_to(eps_a, (VB, VB)).T
        column = turned[pl.ds(pl.multiple_of(a % VB, piece), piece), :]
        for h in range(blocks):
            eps_b = virt[domain[v * blocks + h, j]]
            denominator = (column + eps_b) - occ_energy[i] - occ_energy[j]
            scale[pl.ds(q * piece, piece), slice(h * VB, (h + 1) * VB)] = -1.0 / denominator

    for n in range(SUBS // 2, SUBS):
        for d in (0, 1):
            rs_step(d, 1, RS_ORDER[d][n], True)

    def rs_body(t):
        for n in range(SUBS):
            for d in (0, 1):
                rs_step(d, t, RS_ORDER[d][n], True)

    steps(2, H, rs_body)

    def ag_copy(d, t, sub):
        where = chunk_rows(p - (1 - 2 * d) * t, sub)
        return pltpu.make_async_remote_copy(
            src_ref=amp.at[where, :], dst_ref=amp.at[where, :],
            send_sem=ag_send.at[d, t, sub], recv_sem=ag_recv.at[d, t, sub],
            device_id=target[d], device_id_type=MESH,
        )

    for sub in AG_ORDER:
        for d in (0, 1):
            rs_copy(d, H - 1, sub).wait_recv()
        total = (
            sums[chunk_rows(p, sub), :]
            + came[0, H - 1, part(sub), :].astype(F32)
            + came[1, H - 1, part(sub), :].astype(F32)
        )
        amp[chunk_rows(p, sub), :] = (total * scale[part(sub), :]).astype(BF16)
        for d in (0, 1):
            ag_copy(d, 0, sub).start()

    def ag_body(t):
        for sub in AG_ORDER:
            for d in (0, 1):
                ag_copy(d, t - 1, sub).wait_recv()
                ag_copy(d, t, sub).start()

    steps(1, H - 1, ag_body)
    for sub in AG_ORDER:
        for d in (0, 1):
            ag_copy(d, H - 2, sub).wait_recv()
            if sub in FIRST[d]:
                ag_copy(d, H - 1, sub).start()
    def mul(a, b):
        return jnp.dot(a, b, preferred_element_type=F32)

    def pair_product(k):
        i = jnp.int32(0)
        for m in range(pair_total):
            i = i + (k == m).astype(jnp.int32) * pair_i[m]
        return mul(own[i], amp[half_at(k, 0), :]) + mul(peer[i], amp[half_at(k, 1), :])

    late = pair_total
    start = 0
    if split:
        step = math.gcd(half_rows, half_width)
        late = (half_width - step + half_rows - 1) // half_width + 1
        start = lax.rem(p + H, N) * half_rows // half_width

    def do_pair(n):
        k = lax.rem(jnp.int32(start + n), pair_total)
        products[k] = pair_product(k)

    for n in range(late, pair_total):
        do_pair(n)
    for d in (0, 1):
        for sub in FIRST[d]:
            ag_copy(d, H - 1, sub).wait_recv()

    for n in range(late):
        do_pair(n)
    for j in range(nocc):
        value = products[j]
        for e in range(extras):
            value = value + products[nocc + e] * holds(j, e).astype(F32)
        out[j] = value.astype(BF16)

    for d in (0, 1):
        for sub in FIRST[d]:
            rs_copy(d, 0, sub).wait_send()
            ag_copy(d, H - 1, sub).wait_send()

    def end(t):
        for d in (0, 1):
            for sub in range(SUBS):
                rs_copy(d, t + 1, sub).wait_send()
                ag_copy(d, t, sub).wait_send()

    steps(0, H - 1, end)


def on_device(integrals, virt_energy, occ_energy, domain, partners, pair_count):
    aux_count = lax.axis_size("aux")
    occ_count = lax.axis_size("occ")
    aux_rows, nocc, half_width = integrals.shape
    slot_count = partners.shape[1]
    pair_total = nocc * slot_count * 5 // 8
    width = half_width * lax.axis_size("vir")
    N = aux_count * occ_count
    H = N // 2
    rows = pair_total * width // N
    smem = pl.BlockSpec(memory_space=pltpu.SMEM)
    vmem = pl.BlockSpec(memory_space=pltpu.VMEM)
    gamma = pl.pallas_call(
        functools.partial(kernel, aux_count, occ_count, pair_total),
        out_shape=jax.ShapeDtypeStruct((nocc, aux_rows, half_width), BF16),
        in_specs=[smem] * 4 + [vmem] * 2,
        out_specs=vmem,
        scratch_shapes=[
            pltpu.VMEM((nocc, aux_rows, half_width), BF16),
            pltpu.VMEM((pair_total * width, half_width), F32),
            pltpu.VMEM((pair_total * width, half_width), BF16),
            pltpu.VMEM((2, H, rows, half_width), BF16),
            pltpu.VMEM((2, H, rows, half_width), BF16),
            pltpu.VMEM((VB, VB), F32),
            pltpu.VMEM((rows, half_width), F32),
            pltpu.VMEM((pair_total, aux_rows, half_width), F32),
            pltpu.SemaphoreType.DMA((2,)),
            pltpu.SemaphoreType.DMA((2, H, SUBS)),
            pltpu.SemaphoreType.DMA((2, H, SUBS)),
            pltpu.SemaphoreType.DMA((2, H, SUBS)),
            pltpu.SemaphoreType.DMA((2, H, SUBS)),
        ],
        compiler_params=pltpu.CompilerParams(
            collective_id=0, has_side_effects=True, vmem_limit_bytes=56 * 1024 * 1024,
            allow_input_fusion=[False] * 5 + [True],
        ),
    )(
        partners.T, domain.T, pair_count, occ_energy,
        virt_energy.reshape(-1, 1, VB), jnp.transpose(integrals, (1, 0, 2)),
    )
    return jnp.transpose(gamma, (1, 0, 2))


def solution(mesh):
    in_specs = (
        P(("aux", "occ"), "groups", "vir"),
        P(),
        P("groups"),
        P("groups", None),
        P("groups", None),
        P("groups"),
    )
    out_specs = P(("aux", "occ"), "groups", "vir")
    return jax.shard_map(
        on_device, mesh=mesh, in_specs=in_specs, out_specs=out_specs, check_vma=False
    )
```
